32 devices in a mesh: rep: 4 (over y, x), shard: 8 (over z, core).
Axes of the slice: x: 2, y: 2, z: 4, core: 2. Of those that a mesh axis runs over, the one named last changes fastest.
Arguments:
- slow_weights: float32 [4, 64, 8192], P('rep', 'shard'), may hold values from -0.12 to 0.12
- outer_momentum: float32 [4, 64, 8192], P('rep', 'shard'), may hold values from -0.018 to 0.018
- adam_first: float32 [4, 64, 8192], P('rep', 'shard'), may hold values from -1 to 1
- adam_second: float32 [4, 64, 8192], P('rep', 'shard'), may hold values from 0 to 1, as said below
- gradients: bfloat16 [4, 4, 4, 64, 8192], P(None, None, 'rep', 'shard'), may hold values from -1000 to 1000, as said below
- pair_mask: int32 [4], replicated, may hold values from 1 to 2, as said below
Outputs:
- new_slow: float32 [4, 64, 8192], P('rep', 'shard')
- new_momentum: float32 [4, 64, 8192], P('rep', 'shard')
- new_first: float32 [4, 64, 8192], P('rep', 'shard')
- new_second: float32 [4, 64, 8192], P('rep', 'shard')
The draws below stay inside these ranges and needn't reach their ends.
Inputs may be any that keep to these rules, and one draw needn't show every extreme that they name: In outer step t replica r is matched with replica r XOR pair_mask[t] (bitwise exclusive or); 4 is a power of two, and every pair_mask[t] is a single power of two. Every bit of 3 occurs in some outer step; in which order is drawn anew. `gradients`: gradients of all inner updates. `adam_second`: second moments, positive.
All inputs are finite; a program needn't handle non-finite values.
Results may differ from the reference program's by a relative error of at most 0.0018.
Values may be sent and summed in bfloat16 or wider, within the bound.
A program may use at most 64 MiB of HBM per device.

```python
import math
import jax
import jax.numpy as jnp
from jax import lax

D = 8192
OUTER = 4
INNER = 4
ROWS = 64
REPLICAS = 4


def draw_gradients(key, part):
    keys = jax.random.split(jax.random.fold_in(key, 11), 5)
    shape = (OUTER, INNER, REPLICAS, ROWS, D)
    rising = jnp.exp(math.log(3.0) * jnp.arange(ROWS, dtype=jnp.float32) / ROWS)
    step_scale = jnp.exp(jax.random.uniform(keys[0], (OUTER, INNER, REPLICAS, 1, 1), jnp.float32, math.log(0.3), math.log(3.0)))
    row_scale = jnp.exp(jax.random.uniform(keys[1], (OUTER, INNER, REPLICAS, ROWS, 1), jnp.float32, 0.0, math.log(10.0)))
    values = jnp.clip(jax.random.normal(keys[4], shape, jnp.float32), -4.0, 4.0)
    scaled = jnp.clip(values * step_scale * row_scale * rising[:, None], -1000.0, 1000.0)
    return scaled.astype(jnp.bfloat16)


def draw_adam_first(key, part):
    shape = (REPLICAS, ROWS, D)
    level = 0.3 / math.sqrt(ROWS * D)
    values = jnp.clip(jax.random.normal(jax.random.fold_in(key, 22), shape, jnp.float32), -4.0, 4.0)
    return (values * level).astype(jnp.float32)


def draw_adam_second(key, part):
    shape = (REPLICAS, ROWS, D)
    level = 1.0 / (ROWS * D)
    logs = jax.random.uniform(jax.random.fold_in(key, 32), shape, jnp.float32, math.log(0.1), math.log(10.0))
    return (jnp.exp(logs) * level).astype(jnp.float32)


def draw_pair_mask(key, part):
    bit_count = REPLICAS.bit_length() - 1
    order = jax.random.permutation(jax.random.fold_in(key, 41), bit_count).astype(jnp.int32)
    picks = order[jnp.arange(OUTER, dtype=jnp.int32) % bit_count]
    return jnp.left_shift(jnp.ones((OUTER,), jnp.int32), picks).astype(jnp.int32)


def level_of(key, shape, cuts, smallest, high):
    loudness = 1.0
    for axis_at, parts in cuts:
        draws = jax.random.uniform(jax.random.fold_in(jax.random.fold_in(key, 6), axis_at), (parts,), jnp.float32, smallest / len(cuts), high / len(cuts))
        loudness = loudness * jnp.repeat(jnp.exp(draws), shape[axis_at] // parts).reshape((-1,) + (1,) * (len(shape) - 1 - axis_at))
    return loudness


def normal_values(key, shape, spread, bound, pieces=(), held_as=jnp.bfloat16):
    level = level_of(key, shape, pieces, -0.22, 0.18) if pieces else 1.0
    values = jax.random.normal(key, shape, jnp.float32) * spread * level
    return jnp.minimum(jnp.maximum(values, -bound), bound).astype(held_as)


def setup_inputs(seed: int = 0) -> dict:
    key_of = jax.random.split(jax.random.key(seed), 7)
    return {
        "slow_weights": normal_values(key_of[0], (REPLICAS, ROWS, D), 0.02, 0.12, ((0, 4), (1, 8)), jnp.float32),
        "outer_momentum": normal_values(key_of[1], (REPLICAS, ROWS, D), 0.003, 0.018, ((0, 4), (1, 8)), jnp.float32),
        "adam_first": draw_adam_first(jax.random.fold_in(key_of[6], 71), 0),
        "adam_second": draw_adam_second(jax.random.fold_in(key_of[6], 71), 0),
        "gradients": draw_gradients(jax.random.fold_in(key_of[6], 71), 0),
        "pair_mask": draw_pair_mask(jax.random.fold_in(key_of[6], 71), 0),
    }


clip_limit = 1.0
beta_one = 0.9
beta_two = 0.95
adam_eps = 1e-08
inner_rate = 0.001
decay_rate = 0.1
outer_rate = 0.7
momentum_rate = 0.9
mix_rate = 0.25

def reference(slow_weights, outer_momentum, adam_first, adam_second, gradients, pair_mask):
    slow_now = slow_weights
    momentum = outer_momentum
    moment_one = adam_first
    moment_two = adam_second
    replicas = jnp.arange(REPLICAS, dtype=jnp.int32)
    for outer_step in range(OUTER):
        fast_weights = slow_now
        for inner_step in range(INNER):
            gradient = gradients[outer_step, inner_step].astype(jnp.float32)
            square_sum = lax.optimization_barrier(jnp.sum(gradient * gradient, axis=(1, 2), keepdims=True))
            factor = clip_limit / jnp.maximum(jnp.sqrt(square_sum), clip_limit)
            clipped = factor * gradient
            moment_one = beta_one * moment_one + (1.0 - beta_one) * clipped
            moment_two = beta_two * moment_two + (1.0 - beta_two) * clipped * clipped
            fast_weights = fast_weights - inner_rate * (moment_one / (jnp.sqrt(moment_two) + adam_eps) + decay_rate * fast_weights)
        pseudo_grad = lax.optimization_barrier((slow_now - fast_weights).astype(jnp.bfloat16))
        sent_slow = slow_now.astype(jnp.bfloat16)
        partner = jnp.bitwise_xor(replicas, pair_mask[outer_step]).astype(jnp.int32)
        other_pseudo = jnp.take(pseudo_grad, partner, axis=0).astype(jnp.float32)
        other_slow = jnp.take(sent_slow, partner, axis=0).astype(jnp.float32)
        average = 0.5 * (pseudo_grad.astype(jnp.float32) + other_pseudo)
        momentum = momentum_rate * momentum + average
        slow_now = slow_now + mix_rate * (other_slow - slow_now) - outer_rate * (average + momentum_rate * momentum)
    return (slow_now, momentum, moment_one, moment_two)
```

```python
from functools import partial

import jax
import jax.numpy as jnp
from jax import lax
from jax.experimental import pallas as pl
from jax.experimental.pallas import tpu as pltpu
from jax.sharding import PartitionSpec as P

clip_limit = 1.0
beta_one = 0.9
beta_two = 0.95
adam_eps = 1e-08
inner_rate = 0.001
decay_rate = 0.1
outer_rate = 0.7
momentum_rate = 0.9
mix_rate = 0.25
tiny = 1e-30

LANES = 128
CHUNKS = 4
GROUP = 4
MESH = pl.DeviceIdType.MESH


def shortened(value):

    def short(part):
        return part.astype(jnp.bfloat16) if part.dtype == jnp.float32 else part

    return jax.tree.map(short, value)


def swapped(value, axis, stride):
    mask = 2**stride
    pairs = [(source, source ^ mask) for source in range(lax.axis_size(axis))]
    return lax.ppermute(value, axis, pairs)


def swap_partner(bit_index, payload):
    return jax.tree.map(
        lambda part, own: part.astype(own.dtype),
        swapped(shortened(payload), "rep", bit_index),
        payload,
    )


def step_by_step(slow_weights, outer_momentum, adam_first, adam_second, gradients, pair_mask):
    bit_count = lax.axis_size("rep").bit_length() - 1
    slow_now = slow_weights
    momentum = outer_momentum
    moment_one = adam_first
    moment_two = adam_second
    wide = gradients.astype(jnp.float32)
    square_sums = lax.psum(jnp.sum(wide * wide, axis=(2, 3, 4)), "shard")
    for outer_step in range(gradients.shape[0]):
        fast_weights = slow_now
        for inner_step in range(gradients.shape[1]):
            gradient = gradients[outer_step, inner_step].astype(jnp.float32)
            square_sum = square_sums[outer_step, inner_step]
            factor = clip_limit / jnp.maximum(jnp.sqrt(square_sum), clip_limit)
            clipped = factor * gradient
            moment_one = beta_one * moment_one + (1.0 - beta_one) * clipped
            moment_two = beta_two * moment_two + (1.0 - beta_two) * clipped * clipped
            fast_weights = fast_weights - inner_rate * (
                moment_one / (jnp.sqrt(moment_two) + adam_eps) + decay_rate * fast_weights
            )
        pseudo_grad = (slow_now - fast_weights).astype(jnp.bfloat16)
        sent_slow = slow_now.astype(jnp.bfloat16)
        step_mask = pair_mask[outer_step]
        position = jnp.zeros((), jnp.int32)
        for bit_index in range(bit_count):
            position = position + bit_index * jnp.bitwise_and(
                jnp.right_shift(step_mask, bit_index), 1
            )
        branches = [partial(swap_partner, bit_index) for bit_index in range(bit_count)]
        arrived = lax.switch(position, branches, (pseudo_grad, sent_slow))
        other_pseudo = arrived[0].astype(jnp.float32)
        other_slow = arrived[1].astype(jnp.float32)
        average = 0.5 * (pseudo_grad.astype(jnp.float32) + other_pseudo)
        momentum = momentum_rate * momentum + average
        slow_now = (
            slow_now
            + mix_rate * (other_slow - slow_now)
            - outer_rate * (average + momentum_rate * momentum)
        )
    return (slow_now, momentum, moment_one, moment_two)


def scaled(factor, value):
    return None if value is None else factor * value


def added(left, right):
    if left is None:
        return right
    return left if right is None else left + right


def mixing(step_bits, outer, inner):
    keep = 1.0 - inner_rate * decay_rate
    pull = 1.0 - keep**inner
    one = jnp.ones((8, LANES), jnp.float32)
    spectrum = []
    for char in range(4):
        slow = [one] + [None] * (outer + 1)
        moment = [None, one] + [None] * outer
        for t in range(outer):
            high = step_bits[t]
            differs = (char & 1) * (1.0 - high) + (char >> 1) * high
            same = 1.0 - differs
            half = 1.0 - 2.0 * mix_rate * differs
            average = [scaled(pull * same, part) for part in slow]
            average[2 + t] = same * one
            moment = [
                added(scaled(momentum_rate, part), mean) for part, mean in zip(moment, average)
            ]
            slow = [
                added(
                    scaled(half, part),
                    added(scaled(-outer_rate, mean), scaled(-outer_rate * momentum_rate, push)),
                )
                for part, mean, push in zip(slow, average, moment)
            ]
        spectrum.append((slow, moment))
    table = []
    for d in range(4):
        rows = []
        for output in range(2):
            row = []
            for source in range(outer + 2):
                value = None
                for char in range(4):
                    sign = -0.25 if bin(char & d).count("1") % 2 else 0.25
                    value = added(value, scaled(sign, spectrum[char][output][source]))
                row.append(value)
            rows.append(row)
        table.append(rows)
    return table


def kernel(
    shards,
    mask_ref,
    slow_ref,
    momentum_ref,
    first_ref,
    second_ref,
    grad_ref,
    new_slow_ref,
    new_momentum_ref,
    new_first_ref,
    new_second_ref,
    coef,
    clips,
    sums,
    relay_out,
    relay_in,
    last_out,
    last_in,
    near_out,
    near_in,
    sum_send,
    sum_recv,
    relay_send,
    relay_recv,
    last_send,
    last_recv,
    near_send,
    near_recv,
):
    outer, inner = grad_ref.shape[0], grad_ref.shape[1]
    columns = slow_ref.shape[-1]
    steps = outer * inner
    width = last_out.shape[-1]
    pieces = columns // width
    rep = lax.axis_index("rep")
    shard = lax.axis_index("shard")
    low_partner = rep + 1 - 2 * (rep % 2)
    high_partner = rep + 2 - 4 * ((rep // 2) % 2)

    barrier = pltpu.get_barrier_semaphore()
    for partner in (low_partner, high_partner):
        pl.semaphore_signal(barrier, inc=1, device_id=(partner, shard), device_id_type=MESH)
    for offset in range(1, shards):
        peer = lax.rem(shard + offset, shards)
        pl.semaphore_signal(barrier, inc=1, device_id=(rep, peer), device_id_type=MESH)

    span = LANES * GROUP

    def squares(i, totals):
        totals = list(totals)
        for part in range(GROUP):
            at = pl.ds(pl.multiple_of(i * span + part * LANES, LANES), LANES)
            for j in range(steps):
                grad = grad_ref[j // inner, j % inner, 0, :, at].astype(jnp.float32)
                totals[j] = totals[j] + grad * grad
        return tuple(totals)

    zero = jnp.zeros((8, LANES), jnp.float32)
    totals = lax.fori_loop(0, columns // span, squares, (zero,) * steps)
    lane = lax.broadcasted_iota(jnp.int32, (1, LANES), 1)
    share = jnp.zeros((1, LANES), jnp.float32)
    for j in range(steps):
        column = jnp.sum(totals[j], axis=0, keepdims=True)
        share = jnp.where(lane == j, jnp.sum(column, axis=1, keepdims=True), share)
    sums[0] = share

    pl.semaphore_wait(barrier, shards + 1)
    copies = []
    for offset in range(1, shards):
        peer = lax.rem(shard + offset, shards)
        copies.append(
            pltpu.make_async_remote_copy(
                src_ref=sums.at[0],
                dst_ref=sums.at[offset],
                send_sem=sum_send.at[offset],
                recv_sem=sum_recv.at[offset],
                device_id=(rep, peer),
                device_id_type=MESH,
            )
        )
        copies[-1].start()

    bits = [
        jnp.full((8, LANES), mask_ref[t] - 1, jnp.int32).astype(jnp.float32) for t in range(outer)
    ]
    table = mixing(bits, outer, inner)
    sources = outer + 2
    for d in range(4):
        for output in range(2):
            for source in range(sources):
                coef[(d * 2 + output) * sources + source] = table[d][output][source]

    for copy in copies:
        copy.wait_recv()
    square_sum = sums[0]
    for offset in range(1, shards):
        square_sum = square_sum + sums[offset]
    factor = clip_limit / jnp.maximum(jnp.sqrt(square_sum), clip_limit)
    for j in range(steps):
        clips[j] = jnp.broadcast_to(factor[:, j : j + 1], (8, LANES))

    keep = 1.0 - inner_rate * decay_rate

    def relay(j):
        return pltpu.make_async_remote_copy(
            src_ref=relay_out.at[j],
            dst_ref=relay_in.at[j],
            send_sem=relay_send.at[j],
            recv_sem=relay_recv.at[j],
            device_id=(low_partner + (j % 2) * (high_partner - low_partner), shard),
            device_id_type=MESH,
        )

    def near(j):
        return pltpu.make_async_remote_copy(
            src_ref=near_out.at[j],
            dst_ref=near_in.at[j],
            send_sem=near_send.at[j],
            recv_sem=near_recv.at[j],
            device_id=(low_partner + (j % 2) * (high_partner - low_partner), shard),
            device_id_type=MESH,
        )

    def last(j):
        return pltpu.make_async_remote_copy(
            src_ref=last_out.at[j],
            dst_ref=last_in.at[j],
            send_sem=last_send.at[j],
            recv_sem=last_recv.at[j],
            device_id=(high_partner - (j % 2) * (high_partner - low_partner), shard),
            device_id_type=MESH,
        )

    def updates(j, group):
        base = j * width + group * span
        inside = group * span
        firsts, seconds, moves = [], [], []
        spots = [pl.ds(pl.multiple_of(base + p * LANES, LANES), LANES) for p in range(GROUP)]
        for at in spots:
            firsts.append(first_ref[0, :, at])
            seconds.append(second_ref[0, :, at])
            moves.append([])
        for t in range(outer):
            move = [None] * GROUP
            for k in range(inner):
                clip = clips[t * inner + k]
                gain_one = (1.0 - beta_one) * clip
                gain_two = (1.0 - beta_two) * clip * clip
                for p, at in enumerate(spots):
                    grad = grad_ref[t, k, 0, :, at].astype(jnp.float32)
                    firsts[p] = beta_one * firsts[p] + gain_one * grad
                    seconds[p] = beta_two * seconds[p] + gain_two * (grad * grad)
                    floor = jnp.maximum(seconds[p], tiny)
                    bottom = floor * lax.rsqrt(floor) + adam_eps
                    unit = firsts[p] / bottom
                    move[p] = unit if move[p] is None else keep * move[p] + unit
            for p in range(GROUP):
                moves[p].append(inner_rate * move[p])
        values = []
        for p, at in enumerate(spots):
            new_first_ref[0, :, at] = firsts[p]
            new_second_ref[0, :, at] = seconds[p]
            values.append([slow_ref[0, :, at], momentum_ref[0, :, at]] + moves[p])

        def mixed(d):
            out = []
            for p in range(GROUP):
                pair = []
                for output in range(2):
                    total = None
                    for source in range(sources):
                        weight = coef[(d * 2 + output) * sources + source]
                        total = added(total, weight * values[p][source])
                    pair.append(total)
                out.append(pair)
            return out

        def stored(target, out):
            for p in range(GROUP):
                inside_at = pl.ds(pl.multiple_of(inside + p * LANES, LANES), LANES)
                target[j, :, inside_at] = jnp.concatenate(out[p], axis=0).astype(jnp.bfloat16)

        kind = j % 2
        stored(relay_out, mixed(3))
        stored(near_out, mixed(1 + kind))
        stored(last_out, mixed(2 - kind))
        for (slow, momentum), at in zip(mixed(0), spots):
            new_slow_ref[0, :, at] = slow
            new_momentum_ref[0, :, at] = momentum

    def first_stage(j, carry):

        def body(group, inside):
            updates(j, group)
            return inside

        lax.fori_loop(0, width // span, body, 0)
        relay(j).start()
        near(j).start()
        return carry

    def second_stage(j, carry):
        relay(j).wait_recv()
        last_out[j] = (
            last_out[j].astype(jnp.float32) + relay_in[j].astype(jnp.float32)
        ).astype(jnp.bfloat16)
        last(j).start()
        return carry

    def finish(j, carry):
        near(j).wait_recv()
        last(j).wait_recv()
        at = pl.ds(pl.multiple_of(j * width, LANES), width)
        arrived = near_in[j].astype(jnp.float32) + last_in[j].astype(jnp.float32)
        new_slow_ref[0, :, at] += arrived[:8]
        new_momentum_ref[0, :, at] += arrived[8:]
        return carry

    def both(j, carry):
        first_stage(j, carry)
        return second_stage(j - 2, carry)

    lax.fori_loop(0, 2, first_stage, 0)
    lax.fori_loop(2, pieces, both, 0)
    lax.fori_loop(pieces - 2, pieces, second_stage, 0)
    lax.fori_loop(0, pieces, finish, 0)

    for copy in copies:
        copy.wait_send()

    def drained(j, carry):
        relay(j).wait_send()
        near(j).wait_send()
        last(j).wait_send()
        return carry

    lax.fori_loop(0, pieces, drained, 0)


def four_replicas(slow_weights, outer_momentum, adam_first, adam_second, gradients, pair_mask):
    shards = lax.axis_size("shard")
    outer, inner = gradients.shape[:2]
    columns = slow_weights.shape[-1]
    pieces = 2 * CHUNKS
    width = columns // pieces
    rows = 2 * slow_weights.shape[1]
    piece = pltpu.VMEM((pieces, rows, width), jnp.bfloat16)
    vmem = pl.BlockSpec(memory_space=pltpu.VMEM)
    dma = pltpu.SemaphoreType.DMA
    return pl.pallas_call(
        partial(kernel, shards),
        out_shape=[jax.ShapeDtypeStruct(slow_weights.shape, jnp.float32)] * 4,
        in_specs=[pl.BlockSpec(memory_space=pltpu.SMEM)] + [vmem] * 5,
        out_specs=[vmem] * 4,
        scratch_shapes=[
            pltpu.VMEM((8 * (outer + 2), 8, LANES), jnp.float32),
            pltpu.VMEM((outer * inner, 8, LANES), jnp.float32),
            pltpu.VMEM((shards, 1, LANES), jnp.float32),
            piece,
            piece,
            piece,
            piece,
            piece,
            piece,
            dma((shards,)),
            dma((shards,)),
            dma((pieces,)),
            dma((pieces,)),
            dma((pieces,)),
            dma((pieces,)),
            dma((pieces,)),
            dma((pieces,)),
        ],
        compiler_params=pltpu.CompilerParams(
            collective_id=0, has_side_effects=True, vmem_limit_bytes=32 * 2**20
        ),
    )(pair_mask, slow_weights, outer_momentum, adam_first, adam_second, gradients)


def on_device(*arguments):
    slow_weights, gradients = arguments[0], arguments[4]
    fits = (
        lax.axis_size("rep") == 4
        and slow_weights.shape[:2] == (1, 8)
        and slow_weights.shape[2] % (2 * CHUNKS * GROUP * LANES) == 0
        and gradients.shape[0] * gradients.shape[1] <= LANES
    )
    return four_replicas(*arguments) if fits else step_by_step(*arguments)


def solution(mesh):
    return jax.shard_map(
        on_device,
        mesh=mesh,
        in_specs=(
            P("rep", "shard", None),
            P("rep", "shard", None),
            P("rep", "shard", None),
            P("rep", "shard", None),
            P(None, None, "rep", "shard", None),
            P(),
        ),
        out_specs=(
            P("rep", "shard", None),
            P("rep", "shard", None),
            P("rep", "shard", None),
            P("rep", "shard", None),
        ),
        check_vma=False,
    )
```

```python
from functools import partial

import jax
import jax.numpy as jnp
from jax import lax
from jax.experimental import pallas as pl
from jax.experimental.pallas import tpu as pltpu
from jax.sharding import PartitionSpec as P

clip_limit = 1.0
beta_one = 0.9
beta_two = 0.95
adam_eps = 1e-08
inner_rate = 0.001
decay_rate = 0.1
outer_rate = 0.7
momentum_rate = 0.9
mix_rate = 0.25
tiny = 1e-30

LANES = 128
CHUNKS = 4
GROUP = 8
EARLY = 4
MESH = pl.DeviceIdType.MESH


def shortened(value):

    def short(part):
        return part.astype(jnp.bfloat16) if part.dtype == jnp.float32 else part

    return jax.tree.map(short, value)


def swapped(value, axis, stride):
    mask = 2**stride
    pairs = [(source, source ^ mask) for source in range(lax.axis_size(axis))]
    return lax.ppermute(value, axis, pairs)


def swap_partner(bit_index, payload):
    return jax.tree.map(
        lambda part, own: part.astype(own.dtype),
        swapped(shortened(payload), "rep", bit_index),
        payload,
    )


def step_by_step(slow_weights, outer_momentum, adam_first, adam_second, gradients, pair_mask):
    bit_count = lax.axis_size("rep").bit_length() - 1
    slow_now = slow_weights
    momentum = outer_momentum
    moment_one = adam_first
    moment_two = adam_second
    wide = gradients.astype(jnp.float32)
    square_sums = lax.psum(jnp.sum(wide * wide, axis=(2, 3, 4)), "shard")
    for outer_step in range(gradients.shape[0]):
        fast_weights = slow_now
        for inner_step in range(gradients.shape[1]):
            gradient = gradients[outer_step, inner_step].astype(jnp.float32)
            square_sum = square_sums[outer_step, inner_step]
            factor = clip_limit / jnp.maximum(jnp.sqrt(square_sum), clip_limit)
            clipped = factor * gradient
            moment_one = beta_one * moment_one + (1.0 - beta_one) * clipped
            moment_two = beta_two * moment_two + (1.0 - beta_two) * clipped * clipped
            fast_weights = fast_weights - inner_rate * (
                moment_one / (jnp.sqrt(moment_two) + adam_eps) + decay_rate * fast_weights
            )
        pseudo_grad = (slow_now - fast_weights).astype(jnp.bfloat16)
        sent_slow = slow_now.astype(jnp.bfloat16)
        step_mask = pair_mask[outer_step]
        position = jnp.zeros((), jnp.int32)
        for bit_index in range(bit_count):
            position = position + bit_index * jnp.bitwise_and(
                jnp.right_shift(step_mask, bit_index), 1
            )
        branches = [partial(swap_partner, bit_index) for bit_index in range(bit_count)]
        arrived = lax.switch(position, branches, (pseudo_grad, sent_slow))
        other_pseudo = arrived[0].astype(jnp.float32)
        other_slow = arrived[1].astype(jnp.float32)
        average = 0.5 * (pseudo_grad.astype(jnp.float32) + other_pseudo)
        momentum = momentum_rate * momentum + average
        slow_now = (
            slow_now
            + mix_rate * (other_slow - slow_now)
            - outer_rate * (average + momentum_rate * momentum)
        )
    return (slow_now, momentum, moment_one, moment_two)


def scaled(factor, value):
    return None if value is None else factor * value


def added(left, right):
    if left is None:
        return right
    return left if right is None else left + right


def mixing(step_bits, outer, inner):
    keep = 1.0 - inner_rate * decay_rate
    pull = 1.0 - keep**inner
    one = jnp.ones((8, LANES), jnp.float32)
    spectrum = []
    for char in range(4):
        slow = [one] + [None] * (outer + 1)
        moment = [None, one] + [None] * outer
        for t in range(outer):
            high = step_bits[t]
            differs = (char & 1) * (1.0 - high) + (char >> 1) * high
            same = 1.0 - differs
            half = 1.0 - 2.0 * mix_rate * differs
            average = [scaled(pull * same, part) for part in slow]
            average[2 + t] = same * one
            moment = [
                added(scaled(momentum_rate, part), mean) for part, mean in zip(moment, average)
            ]
            slow = [
                added(
                    scaled(half, part),
                    added(scaled(-outer_rate, mean), scaled(-outer_rate * momentum_rate, push)),
                )
                for part, mean, push in zip(slow, average, moment)
            ]
        spectrum.append((slow, moment))
    table = []
    for d in range(4):
        rows = []
        for output in range(2):
            row = []
            for source in range(outer + 2):
                value = None
                for char in range(4):
                    sign = -0.25 if bin(char & d).count("1") % 2 else 0.25
                    value = added(value, scaled(sign, spectrum[char][output][source]))
                row.append(value)
            rows.append(row)
        table.append(rows)
    return table


def kernel(
    shards,
    mask_ref,
    slow_ref,
    momentum_ref,
    first_ref,
    second_ref,
    grad_ref,
    new_slow_ref,
    new_momentum_ref,
    new_first_ref,
    new_second_ref,
    near_in,
    last_in,
    coef,
    gains,
    sums,
    grads,
    states,
    relay_out,
    relay_in,
    last_sum,
    last_out,
    near_out,
    grad_load,
    state_load,
    sum_send,
    sum_recv,
    relay_send,
    relay_recv,
    last_send,
    last_recv,
    near_send,
    near_recv,
):
    outer, inner = grad_ref.shape[0], grad_ref.shape[1]
    columns = slow_ref.shape[-1]
    steps = outer * inner
    width = last_out.shape[-1]
    pieces = columns // width
    rep = lax.axis_index("rep")
    shard = lax.axis_index("shard")
    low_partner = rep + 1 - 2 * (rep % 2)
    high_partner = rep + 2 - 4 * ((rep // 2) % 2)

    loads = [
        pltpu.make_async_copy(grad_ref.at[t], grads.at[t], grad_load.at[t]) for t in range(outer)
    ]
    for i, ref in enumerate((slow_ref, momentum_ref, first_ref, second_ref)):
        loads.append(pltpu.make_async_copy(ref, states.at[pl.ds(i, 1)], state_load.at[i]))
    for load in loads:
        load.start()

    barrier = pltpu.get_barrier_semaphore()
    for partner in (low_partner, high_partner):
        pl.semaphore_signal(barrier, inc=1, device_id=(partner, shard), device_id_type=MESH)
    for offset in range(1, shards):
        peer = lax.rem(shard + offset, shards)
        pl.semaphore_signal(barrier, inc=1, device_id=(rep, peer), device_id_type=MESH)

    span = LANES * GROUP
    zero = jnp.zeros((8, LANES), jnp.float32)
    totals = []
    for t in range(outer):
        loads[t].wait()

        def squares(i, part_totals, t=t):
            part_totals = list(part_totals)
            for part in range(GROUP):
                at = pl.ds(pl.multiple_of(i * span + part * LANES, LANES), LANES)
                for k in range(inner):
                    grad = grads[t, k, 0, :, at].astype(jnp.float32)
                    part_totals[k] = part_totals[k] + grad * grad
            return tuple(part_totals)

        totals += lax.fori_loop(0, columns // span, squares, (zero,) * inner)
    lane = lax.broadcasted_iota(jnp.int32, (1, LANES), 1)
    share = jnp.zeros((1, LANES), jnp.float32)
    for j in range(steps):
        column = jnp.sum(totals[j], axis=0, keepdims=True)
        share = jnp.where(lane == j, jnp.sum(column, axis=1, keepdims=True), share)
    sums[0] = share

    pl.semaphore_wait(barrier, shards + 1)
    copies = []
    for offset in range(1, shards):
        peer = lax.rem(shard + offset, shards)
        copies.append(
            pltpu.make_async_remote_copy(
                src_ref=sums.at[0],
                dst_ref=sums.at[offset],
                send_sem=sum_send.at[offset],
                recv_sem=sum_recv.at[offset],
                device_id=(rep, peer),
                device_id_type=MESH,
            )
        )
        copies[-1].start()

    bits = [
        jnp.full((8, LANES), mask_ref[t] - 1, jnp.int32).astype(jnp.float32) for t in range(outer)
    ]
    table = mixing(bits, outer, inner)
    sources = outer + 2
    for d in range(4):
        for output in range(2):
            for source in range(sources):
                coef[(d * 2 + output) * sources + source] = table[d][output][source]

    for copy in copies:
        copy.wait_recv()
    square_sum = sums[0]
    for offset in range(1, shards):
        square_sum = square_sum + sums[offset]
    factor = clip_limit / jnp.maximum(jnp.sqrt(square_sum), clip_limit)
    for j in range(steps):
        clip = jnp.broadcast_to(factor[:, j : j + 1], (8, LANES))
        gains[0, j] = (1.0 - beta_one) * clip
        gains[1, j] = (1.0 - beta_two) * clip * clip
    for load in loads[outer:]:
        load.wait()

    keep = 1.0 - inner_rate * decay_rate

    def relay(j):
        return pltpu.make_async_remote_copy(
            src_ref=relay_out.at[j],
            dst_ref=relay_in.at[j],
            send_sem=relay_send.at[j],
            recv_sem=relay_recv.at[j],
            device_id=(low_partner + (j % 2) * (high_partner - low_partner), shard),
            device_id_type=MESH,
        )

    def near(j):
        return pltpu.make_async_remote_copy(
            src_ref=near_out.at[j],
            dst_ref=near_in.at[j],
            send_sem=near_send.at[j],
            recv_sem=near_recv.at[j],
            device_id=(low_partner + (j % 2) * (high_partner - low_partner), shard),
            device_id_type=MESH,
        )

    def last(j):
        return pltpu.make_async_remote_copy(
            src_ref=last_out.at[j],
            dst_ref=last_in.at[j],
            send_sem=last_send.at[j],
            recv_sem=last_recv.at[j],
            device_id=(high_partner - (j % 2) * (high_partner - low_partner), shard),
            device_id_type=MESH,
        )

    def updates(j, group):
        base = j * width + group * span
        inside = group * span
        firsts, seconds, moves = [], [], []
        spots = [pl.ds(pl.multiple_of(base + p * LANES, LANES), LANES) for p in range(GROUP)]
        for at in spots:
            firsts.append(states[2, :, at])
            seconds.append(states[3, :, at])
            moves.append([])
        for t in range(outer):
            move = [None] * GROUP
            for k in range(inner):
                gain_one = gains[0, t * inner + k]
                gain_two = gains[1, t * inner + k]
                for p, at in enumerate(spots):
                    grad = grads[t, k, 0, :, at].astype(jnp.float32)
                    firsts[p] = beta_one * firsts[p] + gain_one * grad
                    seconds[p] = beta_two * seconds[p] + gain_two * (grad * grad)
                    floor = jnp.maximum(seconds[p], tiny)
                    bottom = floor * lax.rsqrt(floor) + adam_eps
                    guess = pl.reciprocal(bottom, approx=True)
                    unit = firsts[p] * (guess * (2.0 - bottom * guess))
                    move[p] = unit if move[p] is None else keep * move[p] + unit
            for p in range(GROUP):
                moves[p].append(inner_rate * move[p])
        values = []
        for p, at in enumerate(spots):
            new_first_ref[0, :, at] = firsts[p]
            new_second_ref[0, :, at] = seconds[p]
            values.append([states[0, :, at], states[1, :, at]] + moves[p])

        def mixed(d):
            out = []
            for p in range(GROUP):
                pair = []
                for output in range(2):
                    total = None
                    for source in range(sources):
                        weight = coef[(d * 2 + output) * sources + source]
                        total = added(total, weight * values[p][source])
                    pair.append(total)
                out.append(pair)
            return out

        def stored(target, out):
            for p in range(GROUP):
                inside_at = pl.ds(pl.multiple_of(inside + p * LANES, LANES), LANES)
                both = jnp.concatenate(out[p], axis=0)
                target[j, :, inside_at] = both.astype(target.dtype)

        kind = j % 2
        stored(relay_out, mixed(3))
        stored(near_out, mixed(1 + kind))
        stored(last_sum, mixed(2 - kind))
        for (slow, momentum), at in zip(mixed(0), spots):
            new_slow_ref[0, :, at] = slow
            new_momentum_ref[0, :, at] = momentum

    def first_stage(j, carry):

        def body(group, inside):
            updates(j, group)
            return inside

        lax.fori_loop(0, width // span, body, 0)
        relay(j).start()
        return carry

    def first_stage_and_near(j, carry):
        first_stage(j, carry)
        near(j).start()
        return carry

    def second_stage(j, carry):
        relay(j).wait_recv()
        last_out[j] = (last_sum[j] + relay_in[j].astype(jnp.float32)).astype(jnp.bfloat16)
        last(j).start()
        return carry

    def near_stage(j, carry):
        near(j).start()
        return carry

    def finish(j, carry):
        near(j).wait_recv()
        last(j).wait_recv()
        return carry

    early = min(EARLY, pieces)
    lax.fori_loop(0, early, first_stage_and_near, 0)
    lax.fori_loop(early, pieces, first_stage, 0)
    lax.fori_loop(0, pieces, second_stage, 0)
    lax.fori_loop(early, pieces, near_stage, 0)
    lax.fori_loop(0, pieces, finish, 0)

    for copy in copies:
        copy.wait_send()

    def drained(j, carry):
        relay(j).wait_send()
        near(j).wait_send()
        last(j).wait_send()
        return carry

    lax.fori_loop(0, pieces, drained, 0)


def finish_kernel(
    slow_ref,
    momentum_ref,
    first_ref,
    second_ref,
    near_ref,
    last_ref,
    new_slow_ref,
    new_momentum_ref,
    new_first_ref,
    new_second_ref,
    slow,
    momentum,
    stored,
):
    pieces, rows, width = near_ref.shape
    copies = [
        pltpu.make_async_copy(first_ref, new_first_ref, stored.at[0]),
        pltpu.make_async_copy(second_ref, new_second_ref, stored.at[1]),
    ]
    for copy in copies:
        copy.start()

    def add(j, carry):
        at = pl.ds(pl.multiple_of(j * width, LANES), width)
        arrived = near_ref[j].astype(jnp.float32) + last_ref[j].astype(jnp.float32)
        slow[0, :, at] = slow_ref[0, :, at] + arrived[: rows // 2]
        momentum[0, :, at] = momentum_ref[0, :, at] + arrived[rows // 2 :]
        return carry

    lax.fori_loop(0, pieces, add, 0)
    for i, (value, target) in enumerate(((slow, new_slow_ref), (momentum, new_momentum_ref))):
        copies.append(pltpu.make_async_copy(value, target, stored.at[2 + i]))
        copies[-1].start()
    for copy in copies:
        copy.wait()


def four_replicas(slow_weights, outer_momentum, adam_first, adam_second, gradients, pair_mask):
    shards = lax.axis_size("shard")
    outer, inner = gradients.shape[:2]
    _, rows, columns = slow_weights.shape
    pieces = 2 * CHUNKS
    piece = (pieces, 2 * rows, columns // pieces)
    half = pltpu.VMEM(piece, jnp.bfloat16)
    vmem = pl.BlockSpec(memory_space=pltpu.VMEM)
    hbm = pl.BlockSpec(memory_space=pltpu.HBM)
    dma = pltpu.SemaphoreType.DMA
    slab = jax.ShapeDtypeStruct(slow_weights.shape, jnp.float32)
    parts = pl.pallas_call(
        partial(kernel, shards),
        out_shape=[slab] * 4 + [jax.ShapeDtypeStruct(piece, jnp.bfloat16)] * 2,
        in_specs=[pl.BlockSpec(memory_space=pltpu.SMEM)] + [hbm] * 5,
        out_specs=[vmem] * 6,
        scratch_shapes=[
            pltpu.VMEM((8 * (outer + 2), 8, LANES), jnp.float32),
            pltpu.VMEM((2, outer * inner, 8, LANES), jnp.float32),
            pltpu.VMEM((shards, 1, LANES), jnp.float32),
            pltpu.VMEM(gradients.shape, gradients.dtype),
            pltpu.VMEM((4, rows, columns), jnp.float32),
            half,
            half,
            pltpu.VMEM(piece, jnp.float32),
            half,
            half,
            dma((outer,)),
            dma((4,)),
            dma((shards,)),
            dma((shards,)),
            dma((pieces,)),
            dma((pieces,)),
            dma((pieces,)),
            dma((pieces,)),
            dma((pieces,)),
            dma((pieces,)),
        ],
        compiler_params=pltpu.CompilerParams(
            collective_id=0, has_side_effects=True, vmem_limit_bytes=54980608
        ),
    )(pair_mask, slow_weights, outer_momentum, adam_first, adam_second, gradients)
    return pl.pallas_call(
        finish_kernel,
        out_shape=[slab] * 4,
        in_specs=[vmem] * 6,
        out_specs=[hbm] * 4,
        scratch_shapes=[
            pltpu.VMEM(slab.shape, jnp.float32),
            pltpu.VMEM(slab.shape, jnp.float32),
            dma((4,)),
        ],
        compiler_params=pltpu.CompilerParams(vmem_limit_bytes=16 * 2**20),
    )(*parts)


def on_device(*arguments):
    slow_weights, gradients = arguments[0], arguments[4]
    fits = (
        lax.axis_size("rep") == 4
        and slow_weights.shape[:2] == (1, 8)
        and slow_weights.shape[2] % (2 * CHUNKS * GROUP * LANES) == 0
        and gradients.shape[0] * gradients.shape[1] <= LANES
    )
    return four_replicas(*arguments) if fits else step_by_step(*arguments)


def solution(mesh):
    return jax.shard_map(
        on_device,
        mesh=mesh,
        in_specs=(
            P("rep", "shard", None),
            P("rep", "shard", None),
            P("rep", "shard", None),
            P("rep", "shard", None),
            P(None, None, "rep", "shard", None),
            P(),
        ),
        out_specs=(
            P("rep", "shard", None),
            P("rep", "shard", None),
            P("rep", "shard", None),
            P("rep", "shard", None),
        ),
        check_vma=False,
    )
```

```python
from functools import partial

import jax
import jax.numpy as jnp
from jax import lax
from jax.experimental import pallas as pl
from jax.experimental.pallas import tpu as pltpu
from jax.sharding import PartitionSpec as P

clip_limit = 1.0
beta_one = 0.9
beta_two = 0.95
adam_eps = 1e-08
inner_rate = 0.001
decay_rate = 0.1
outer_rate = 0.7
momentum_rate = 0.9
mix_rate = 0.25
tiny = 1e-30

LANES = 128
CHUNKS = 4
GROUP = 8
EARLY = 4
MESH = pl.DeviceIdType.MESH


def shortened(value):

    def short(part):
        return part.astype(jnp.bfloat16) if part.dtype == jnp.float32 else part

    return jax.tree.map(short, value)


def swapped(value, axis, stride):
    mask = 2**stride
    pairs = [(source, source ^ mask) for source in range(lax.axis_size(axis))]
    return lax.ppermute(value, axis, pairs)


def swap_partner(bit_index, payload):
    return jax.tree.map(
        lambda part, own: part.astype(own.dtype),
        swapped(shortened(payload), "rep", bit_index),
        payload,
    )


def step_by_step(slow_weights, outer_momentum, adam_first, adam_second, gradients, pair_mask):
    bit_count = lax.axis_size("rep").bit_length() - 1
    slow_now = slow_weights
    momentum = outer_momentum
    moment_one = adam_first
    moment_two = adam_second
    wide = gradients.astype(jnp.float32)
    square_sums = lax.psum(jnp.sum(wide * wide, axis=(2, 3, 4)), "shard")
    for outer_step in range(gradients.shape[0]):
        fast_weights = slow_now
        for inner_step in range(gradients.shape[1]):
            gradient = gradients[outer_step, inner_step].astype(jnp.float32)
            square_sum = square_sums[outer_step, inner_step]
            factor = clip_limit / jnp.maximum(jnp.sqrt(square_sum), clip_limit)
            clipped = factor * gradient
            moment_one = beta_one * moment_one + (1.0 - beta_one) * clipped
            moment_two = beta_two * moment_two + (1.0 - beta_two) * clipped * clipped
            fast_weights = fast_weights - inner_rate * (
                moment_one / (jnp.sqrt(moment_two) + adam_eps) + decay_rate * fast_weights
            )
        pseudo_grad = (slow_now - fast_weights).astype(jnp.bfloat16)
        sent_slow = slow_now.astype(jnp.bfloat16)
        step_mask = pair_mask[outer_step]
        position = jnp.zeros((), jnp.int32)
        for bit_index in range(bit_count):
            position = position + bit_index * jnp.bitwise_and(
                jnp.right_shift(step_mask, bit_index), 1
            )
        branches = [partial(swap_partner, bit_index) for bit_index in range(bit_count)]
        arrived = lax.switch(position, branches, (pseudo_grad, sent_slow))
        other_pseudo = arrived[0].astype(jnp.float32)
        other_slow = arrived[1].astype(jnp.float32)
        average = 0.5 * (pseudo_grad.astype(jnp.float32) + other_pseudo)
        momentum = momentum_rate * momentum + average
        slow_now = (
            slow_now
            + mix_rate * (other_slow - slow_now)
            - outer_rate * (average + momentum_rate * momentum)
        )
    return (slow_now, momentum, moment_one, moment_two)


def scaled(factor, value):
    return None if value is None else factor * value


def added(left, right):
    if left is None:
        return right
    return left if right is None else left + right


def mixing(step_bits, outer, inner):
    keep = 1.0 - inner_rate * decay_rate
    pull = 1.0 - keep**inner
    one = jnp.ones((8, LANES), jnp.float32)
    spectrum = []
    for char in range(4):
        slow = [one] + [None] * (outer + 1)
        moment = [None, one] + [None] * outer
        for t in range(outer):
            high = step_bits[t]
            differs = (char & 1) * (1.0 - high) + (char >> 1) * high
            same = 1.0 - differs
            half = 1.0 - 2.0 * mix_rate * differs
            average = [scaled(pull * same, part) for part in slow]
            average[2 + t] = same * one
            moment = [
                added(scaled(momentum_rate, part), mean) for part, mean in zip(moment, average)
            ]
            slow = [
                added(
                    scaled(half, part),
                    added(scaled(-outer_rate, mean), scaled(-outer_rate * momentum_rate, push)),
                )
                for part, mean, push in zip(slow, average, moment)
            ]
        spectrum.append((slow, moment))
    table = []
    for d in range(4):
        rows = []
        for output in range(2):
            row = []
            for source in range(outer + 2):
                value = None
                for char in range(4):
                    sign = -0.25 if bin(char & d).count("1") % 2 else 0.25
                    value = added(value, scaled(sign, spectrum[char][output][source]))
                row.append(value)
            rows.append(row)
        table.append(rows)
    return table


def kernel(
    shards,
    mask_ref,
    slow_ref,
    momentum_ref,
    first_ref,
    second_ref,
    grad_ref,
    new_slow_ref,
    new_momentum_ref,
    new_first_ref,
    new_second_ref,
    near_in,
    last_in,
    coef,
    gains,
    sums,
    grads,
    states,
    relay_out,
    relay_in,
    last_sum,
    last_out,
    near_out,
    grad_load,
    state_load,
    sum_send,
    sum_recv,
    relay_send,
    relay_recv,
    last_send,
    last_recv,
    near_send,
    near_recv,
):
    outer, inner = grad_ref.shape[0], grad_ref.shape[1]
    columns = slow_ref.shape[-1]
    steps = outer * inner
    width = last_out.shape[-1]
    pieces = columns // width
    rep = lax.axis_index("rep")
    shard = lax.axis_index("shard")
    low_partner = rep + 1 - 2 * (rep % 2)
    high_partner = rep + 2 - 4 * ((rep // 2) % 2)

    loads = [
        pltpu.make_async_copy(grad_ref.at[t], grads.at[t], grad_load.at[t]) for t in range(outer)
    ]
    for i, ref in enumerate((slow_ref, momentum_ref, first_ref, second_ref)):
        loads.append(pltpu.make_async_copy(ref, states.at[pl.ds(i, 1)], state_load.at[i]))
    for load in loads:
        load.start()

    barrier = pltpu.get_barrier_semaphore()
    for partner in (low_partner, high_partner):
        pl.semaphore_signal(barrier, inc=1, device_id=(partner, shard), device_id_type=MESH)
    for offset in range(1, shards):
        peer = lax.rem(shard + offset, shards)
        pl.semaphore_signal(barrier, inc=1, device_id=(rep, peer), device_id_type=MESH)

    span = LANES * GROUP
    zero = jnp.zeros((8, LANES), jnp.float32)
    totals = []
    for t in range(outer):
        loads[t].wait()

        def squares(i, part_totals, t=t):
            part_totals = list(part_totals)
            for part in range(GROUP):
                at = pl.ds(pl.multiple_of(i * span + part * LANES, LANES), LANES)
                for k in range(inner):
                    grad = grads[t, k, 0, :, at].astype(jnp.float32)
                    part_totals[k] = part_totals[k] + grad * grad
            return tuple(part_totals)

        totals += lax.fori_loop(0, columns // span, squares, (zero,) * inner)
    lane = lax.broadcasted_iota(jnp.int32, (1, LANES), 1)
    share = jnp.zeros((1, LANES), jnp.float32)
    for j in range(steps):
        column = jnp.sum(totals[j], axis=0, keepdims=True)
        share = jnp.where(lane == j, jnp.sum(column, axis=1, keepdims=True), share)
    sums[0] = share

    pl.semaphore_wait(barrier, shards + 1)
    copies = []
    for offset in range(1, shards):
        peer = lax.rem(shard + offset, shards)
        copies.append(
            pltpu.make_async_remote_copy(
                src_ref=sums.at[0],
                dst_ref=sums.at[offset],
                send_sem=sum_send.at[offset],
                recv_sem=sum_recv.at[offset],
                device_id=(rep, peer),
                device_id_type=MESH,
            )
        )
        copies[-1].start()

    bits = [
        jnp.full((8, LANES), mask_ref[t] - 1, jnp.int32).astype(jnp.float32) for t in range(outer)
    ]
    table = mixing(bits, outer, inner)
    sources = outer + 2
    for d in range(4):
        for output in range(2):
            for source in range(sources):
                coef[(d * 2 + output) * sources + source] = table[d][output][source]

    for copy in copies:
        copy.wait_recv()
    square_sum = sums[0]
    for offset in range(1, shards):
        square_sum = square_sum + sums[offset]
    factor = clip_limit / jnp.maximum(jnp.sqrt(square_sum), clip_limit)
    for j in range(steps):
        clip = jnp.broadcast_to(factor[:, j : j + 1], (8, LANES))
        gains[0, j] = (1.0 - beta_one) * clip
        gains[1, j] = (1.0 - beta_two) * clip * clip
    for load in loads[outer:]:
        load.wait()

    keep = 1.0 - inner_rate * decay_rate

    def relay(j):
        return pltpu.make_async_remote_copy(
            src_ref=relay_out.at[j],
            dst_ref=relay_in.at[j],
            send_sem=relay_send.at[j],
            recv_sem=relay_recv.at[j],
            device_id=(low_partner + ((j + shard) % 2) * (high_partner - low_partner), shard),
            device_id_type=MESH,
        )

    def near(j):
        return pltpu.make_async_remote_copy(
            src_ref=near_out.at[j],
            dst_ref=near_in.at[j],
            send_sem=near_send.at[j],
            recv_sem=near_recv.at[j],
            device_id=(low_partner + ((j + shard) % 2) * (high_partner - low_partner), shard),
            device_id_type=MESH,
        )

    def last(j):
        return pltpu.make_async_remote_copy(
            src_ref=last_out.at[j],
            dst_ref=last_in.at[j],
            send_sem=last_send.at[j],
            recv_sem=last_recv.at[j],
            device_id=(high_partner - ((j + shard) % 2) * (high_partner - low_partner), shard),
            device_id_type=MESH,
        )

    def updates(j, group):
        base = j * width + group * span
        inside = group * span
        firsts, seconds, moves = [], [], []
        spots = [pl.ds(pl.multiple_of(base + p * LANES, LANES), LANES) for p in range(GROUP)]
        for at in spots:
            firsts.append(states[2, :, at])
            seconds.append(states[3, :, at])
            moves.append([])
        for t in range(outer):
            move = [None] * GROUP
            for k in range(inner):
                gain_one = gains[0, t * inner + k]
                gain_two = gains[1, t * inner + k]
                for p, at in enumerate(spots):
                    grad = grads[t, k, 0, :, at].astype(jnp.float32)
                    firsts[p] = beta_one * firsts[p] + gain_one * grad
                    seconds[p] = beta_two * seconds[p] + gain_two * (grad * grad)
                    floor = jnp.maximum(seconds[p], tiny)
                    bottom = floor * lax.rsqrt(floor) + adam_eps
                    guess = pl.reciprocal(bottom, approx=True)
                    unit = firsts[p] * (guess * (2.0 - bottom * guess))
                    move[p] = unit if move[p] is None else keep * move[p] + unit
            for p in range(GROUP):
                moves[p].append(inner_rate * move[p])
        values = []
        for p, at in enumerate(spots):
            new_first_ref[0, :, at] = firsts[p]
            new_second_ref[0, :, at] = seconds[p]
            values.append([states[0, :, at], states[1, :, at]] + moves[p])

        def mixed(d):
            out = []
            for p in range(GROUP):
                pair = []
                for output in range(2):
                    total = None
                    for source in range(sources):
                        weight = coef[(d * 2 + output) * sources + source]
                        total = added(total, weight * values[p][source])
                    pair.append(total)
                out.append(pair)
            return out

        def stored(target, out):
            for p in range(GROUP):
                inside_at = pl.ds(pl.multiple_of(inside + p * LANES, LANES), LANES)
                both = jnp.concatenate(out[p], axis=0)
                target[j, :, inside_at] = both.astype(target.dtype)

        kind = (j + shard) % 2
        stored(relay_out, mixed(3))
        stored(near_out, mixed(1 + kind))
        stored(last_sum, mixed(2 - kind))
        for (slow, momentum), at in zip(mixed(0), spots):
            new_slow_ref[0, :, at] = slow
            new_momentum_ref[0, :, at] = momentum

    def first_stage(j, carry):

        def body(group, inside):
            updates(j, group)
            return inside

        lax.fori_loop(0, width // span, body, 0)
        relay(j).start()
        return carry

    def first_stage_and_near(j, carry):
        first_stage(j, carry)
        near(j).start()
        return carry

    def second_stage(j, carry):
        relay(j).wait_recv()
        last_out[j] = (last_sum[j] + relay_in[j].astype(jnp.float32)).astype(jnp.bfloat16)
        last(j).start()
        return carry

    def near_stage(j, carry):
        near(j).start()
        return carry

    def finish(j, carry):
        near(j).wait_recv()
        last(j).wait_recv()
        return carry

    early = min(EARLY, pieces)
    lax.fori_loop(0, early, first_stage_and_near, 0)
    lax.fori_loop(early, pieces, first_stage, 0)
    lax.fori_loop(0, pieces, second_stage, 0)
    lax.fori_loop(early, pieces, near_stage, 0)
    lax.fori_loop(0, pieces, finish, 0)

    for copy in copies:
        copy.wait_send()

    def drained(j, carry):
        relay(j).wait_send()
        near(j).wait_send()
        last(j).wait_send()
        return carry

    lax.fori_loop(0, pieces, drained, 0)


def finish_kernel(
    slow_ref,
    momentum_ref,
    first_ref,
    second_ref,
    near_ref,
    last_ref,
    new_slow_ref,
    new_momentum_ref,
    new_first_ref,
    new_second_ref,
    slow,
    momentum,
    stored,
):
    pieces, rows, width = near_ref.shape
    copies = [
        pltpu.make_async_copy(first_ref, new_first_ref, stored.at[0]),
        pltpu.make_async_copy(second_ref, new_second_ref, stored.at[1]),
    ]
    for copy in copies:
        copy.start()

    def add(j, carry):
        at = pl.ds(pl.multiple_of(j * width, LANES), width)
        arrived = near_ref[j].astype(jnp.float32) + last_ref[j].astype(jnp.float32)
        slow[0, :, at] = slow_ref[0, :, at] + arrived[: rows // 2]
        momentum[0, :, at] = momentum_ref[0, :, at] + arrived[rows // 2 :]
        return carry

    lax.fori_loop(0, pieces, add, 0)
    for i, (value, target) in enumerate(((slow, new_slow_ref), (momentum, new_momentum_ref))):
        copies.append(pltpu.make_async_copy(value, target, stored.at[2 + i]))
        copies[-1].start()
    for copy in copies:
        copy.wait()


def four_replicas(slow_weights, outer_momentum, adam_first, adam_second, gradients, pair_mask):
    shards = lax.axis_size("shard")
    outer, inner = gradients.shape[:2]
    _, rows, columns = slow_weights.shape
    pieces = 2 * CHUNKS
    piece = (pieces, 2 * rows, columns // pieces)
    half = pltpu.VMEM(piece, jnp.bfloat16)
    vmem = pl.BlockSpec(memory_space=pltpu.VMEM)
    hbm = pl.BlockSpec(memory_space=pltpu.HBM)
    dma = pltpu.SemaphoreType.DMA
    slab = jax.ShapeDtypeStruct(slow_weights.shape, jnp.float32)
    parts = pl.pallas_call(
        partial(kernel, shards),
        out_shape=[slab] * 4 + [jax.ShapeDtypeStruct(piece, jnp.bfloat16)] * 2,
        in_specs=[pl.BlockSpec(memory_space=pltpu.SMEM)] + [hbm] * 5,
        out_specs=[vmem] * 6,
        scratch_shapes=[
            pltpu.VMEM((8 * (outer + 2), 8, LANES), jnp.float32),
            pltpu.VMEM((2, outer * inner, 8, LANES), jnp.float32),
            pltpu.VMEM((shards, 1, LANES), jnp.float32),
            pltpu.VMEM(gradients.shape, gradients.dtype),
            pltpu.VMEM((4, rows, columns), jnp.float32),
            half,
            half,
            pltpu.VMEM(piece, jnp.float32),
            half,
            half,
            dma((outer,)),
            dma((4,)),
            dma((shards,)),
            dma((shards,)),
            dma((pieces,)),
            dma((pieces,)),
            dma((pieces,)),
            dma((pieces,)),
            dma((pieces,)),
            dma((pieces,)),
        ],
        compiler_params=pltpu.CompilerParams(
            collective_id=0, has_side_effects=True, vmem_limit_bytes=54980608
        ),
    )(pair_mask, slow_weights, outer_momentum, adam_first, adam_second, gradients)
    return pl.pallas_call(
        finish_kernel,
        out_shape=[slab] * 4,
        in_specs=[vmem] * 6,
        out_specs=[hbm] * 4,
        scratch_shapes=[
            pltpu.VMEM(slab.shape, jnp.float32),
            pltpu.VMEM(slab.shape, jnp.float32),
            dma((4,)),
        ],
        compiler_params=pltpu.CompilerParams(vmem_limit_bytes=16 * 2**20),
    )(*parts)


def on_device(*arguments):
    slow_weights, gradients = arguments[0], arguments[4]
    fits = (
        lax.axis_size("rep") == 4
        and slow_weights.shape[:2] == (1, 8)
        and slow_weights.shape[2] % (2 * CHUNKS * GROUP * LANES) == 0
        and gradients.shape[0] * gradients.shape[1] <= LANES
    )
    return four_replicas(*arguments) if fits else step_by_step(*arguments)


def solution(mesh):
    return jax.shard_map(
        on_device,
        mesh=mesh,
        in_specs=(
            P("rep", "shard", None),
            P("rep", "shard", None),
            P("rep", "shard", None),
            P("rep", "shard", None),
            P(None, None, "rep", "shard", None),
            P(),
        ),
        out_specs=(
            P("rep", "shard", None),
            P("rep", "shard", None),
            P("rep", "shard", None),
            P("rep", "shard", None),
        ),
        check_vma=False,
    )
```
